256 devices in a mesh: expert: 32 (over x, z_lo, core), dp: 8 (over z_hi, y).
Axes of the slice: x: 4, y: 4, z: 8 (z_hi: 2, z_lo: 4; z = z_hi * 4 + z_lo), core: 2. Of those that a mesh axis runs over, the one named last changes fastest.
Arguments:
- tokens_a: bfloat16 [16384, 2048], P(('expert', 'dp')), may hold values from -6 to 6
- cotangent_a: bfloat16 [16384, 2048], P(('expert', 'dp')), may hold values from -6 to 6
- route_a: int32 [16384, 8], P(('expert', 'dp')), may hold values from 0 to 31, all different within a row; in each aligned block of 64 rows (0 to 63, 64 to 127, ...) at most 20 rows name the same one
- gate_a: float32 [16384, 8], P(('expert', 'dp')), may hold values from 0.05 to 0.3
- tokens_b: bfloat16 [16384, 2048], P(('expert', 'dp')), may hold values from -6 to 6
- route_b: int32 [16384, 8], P(('expert', 'dp')), may hold values from 0 to 31, all different within a row; in each aligned block of 64 rows (0 to 63, 64 to 127, ...) at most 20 rows name the same one
- gate_b: float32 [16384, 8], P(('expert', 'dp')), may hold values from 0.05 to 0.3
- w_gate_up: bfloat16 [32, 2048, 1024], P('expert'), may hold values from -0.125 to 0.125
- w_down: bfloat16 [32, 2048, 512], P('expert'), may hold values from -0.25 to 0.25
Outputs:
- input_grad: bfloat16 [16384, 2048], P(('expert', 'dp'))
- mixed: bfloat16 [16384, 2048], P(('expert', 'dp'))
- grad_gate_up: float32 [32, 2048, 1024], P('expert', 'dp')
- grad_down: float32 [32, 2048, 512], P('expert', 'dp')
The draws below stay inside these ranges and needn't reach their ends.
Inputs may be any that keep to these rules, and one draw needn't show every extreme that they name: `route_a`: among the rows of one device, no expert is named more than 20 times. `route_b`: among the rows of one device, no expert is named more than 20 times.
All inputs are finite; a program needn't handle non-finite values.
Results may differ from the reference program's by a relative error of at most 0.014.
Values may be sent and summed in bfloat16 or wider, within the bound.
No kernel may reach another device: no remote copies, remote signals or barrier semaphores. Data moves between devices by JAX's collectives and lax.ppermute only.
A program may use at most 128 MiB of HBM per device.

```python
import math
from functools import partial
import jax
import jax.numpy as jnp
import numpy as np
from jax import lax

D = 2048
FF = 512
TOP = 8
TOK_DEV = 64
EXPERTS = 32
CAP = 20
TOKENS = 16384
N_EXPERT = 32
N_DP = 8


def levels(own_key, shape, pieces, low, largest):
    gain = 1.0
    for axis_at, parts in pieces:
        draws = jax.random.uniform(jax.random.fold_in(jax.random.fold_in(own_key, 6), axis_at), (parts,), jnp.float32, low / len(pieces), largest / len(pieces))
        gain = gain * jnp.repeat(jnp.exp(draws), shape[axis_at] // parts).reshape((-1,) + (1,) * (len(shape) - 1 - axis_at))
    return gain


def routed_block(rng, own, number, rows, amount, top, reach, lean):
    ranking = jax.random.permutation(rng, amount)
    packed, common = shares(amount, rows * top, reach, lean, True), shares(amount, rows * top, reach, lean, False)
    places = jnp.arange(amount)

    def named(lengths, offset_by):
        used = int((lengths > 0).sum())
        fixed = max(1, used // 4)
        shifted = fixed + (places - fixed + offset_by * (used - fixed)) % max(1, amount - fixed)
        return jnp.zeros((amount,), jnp.int32).at[ranking[jnp.where(places < fixed, places, shifted)]].set(jnp.asarray(lengths, jnp.int32))

    lengths = jnp.where(number % 4 == 0, named(packed, number // 4), named(common, number - number // 4 - 1))
    mixed = jax.random.permutation(jax.random.fold_in(own, 3), amount)
    giver, taker = mixed[0:amount // 2 * 2:2], mixed[1:amount // 2 * 2:2]
    margin = jnp.minimum(lengths[giver] - 1, reach - lengths[taker]) // 2
    margin = jnp.where((giver == ranking[0]) | (taker == ranking[0]) | (lengths[taker] == 0), 0, jnp.maximum(margin, 0))
    shifted = jax.random.randint(jax.random.fold_in(own, 4), (amount // 2,), 0, 1 << 20) % (margin + 1)
    lengths = lengths.at[giver].add(-shifted).at[taker].add(shifted)
    members = jnp.searchsorted(jnp.cumsum(lengths), jnp.arange(rows * top), side="right").astype(jnp.int32)
    grid = members.reshape(top, rows).T
    grid = grid[jax.random.permutation(jax.random.fold_in(own, 1), rows)]
    offset_by = jax.random.randint(jax.random.fold_in(own, 2), (rows, 1), 0, top)
    return jnp.take_along_axis(grid, (jnp.arange(top)[None, :] + offset_by) % top, axis=1)


def shares(number_of, total, reach, slope, full):
    loads = [(1 << 20) // math.isqrt(grade ** slope) + 1 for grade in range(1, number_of + 1)]
    largest = reach if full else min(reach, max(-(-total // number_of), total * loads[0] // sum(loads)))
    least = 1 if total - largest >= number_of - 1 else 0
    given, rest = [largest] + [least] * (number_of - 1), total - largest - least * (number_of - 1)
    while rest > 0:
        movable = [i for i in range(1, number_of) if given[i] < largest] or [i for i in range(1, number_of) if given[i] < reach]
        mass, remaining = sum([loads[i] for i in movable]), rest
        for i in movable:
            addition = min(reach - given[i], max(1, remaining * loads[i] // mass), rest)
            given[i] = given[i] + addition
            rest = rest - addition
    return np.array(given)


def gaussian(own_key, extent, width, bound, shards=(), kind=jnp.bfloat16):
    entries = jax.random.normal(own_key, extent, jnp.float32) * width
    if len(shards) > 0:
        entries = levels(own_key, extent, shards, -0.22, 0.18) * entries
    return jnp.clip(entries, min=-bound, max=bound).astype(kind)


def setup_inputs(seed: int = 0) -> dict:
    key_list = jax.random.split(jax.random.key(seed), 10)
    tokens_a = gaussian(key_list[0], (TOKENS, D), 1.0, 6.0, ((0, 256),))
    cotangent_a = gaussian(key_list[1], (TOKENS, D), 1.0, 6.0, ((0, 256),))
    route_a_keys = jax.random.split(jax.random.fold_in(key_list[2], 1), TOKENS // TOK_DEV)
    route_a_turns = jax.random.permutation(jax.random.fold_in(key_list[2], 3), TOKENS // TOK_DEV)
    route_a = jax.vmap(lambda own, number: routed_block(jax.random.fold_in(key_list[2], 2), own, number, TOK_DEV, EXPERTS, TOP, CAP, 2))(route_a_keys, route_a_turns).reshape((TOKENS, TOP))
    gate_a = jnp.clip(0.05 + 0.25 * jax.random.uniform(key_list[3], (TOKENS, TOP), jnp.float32) ** levels(key_list[3], (TOKENS, TOP), ((0, 256),), -0.2, 0.2), 0.05, 0.3)
    tokens_b = gaussian(key_list[4], (TOKENS, D), 1.0, 6.0, ((0, 256),))
    route_b_keys = jax.random.split(jax.random.fold_in(key_list[5], 1), TOKENS // TOK_DEV)
    route_b_turns = jax.random.permutation(jax.random.fold_in(key_list[5], 3), TOKENS // TOK_DEV)
    route_b = jax.vmap(lambda own, number: routed_block(jax.random.fold_in(key_list[5], 2), own, number, TOK_DEV, EXPERTS, TOP, CAP, 2))(route_b_keys, route_b_turns).reshape((TOKENS, TOP))
    gate_b = jnp.clip(0.05 + 0.25 * jax.random.uniform(key_list[6], (TOKENS, TOP), jnp.float32) ** levels(key_list[6], (TOKENS, TOP), ((0, 256),), -0.2, 0.2), 0.05, 0.3)
    w_gate_up = gaussian(key_list[7], (EXPERTS, D, 2 * FF), D ** -0.5, 0.125, ((0, 32),))
    w_down = gaussian(key_list[8], (EXPERTS, D, FF), FF ** -0.5, 0.25, ((0, 32),))
    return {"tokens_a": tokens_a, "cotangent_a": cotangent_a, "route_a": route_a, "gate_a": gate_a, "tokens_b": tokens_b, "route_b": route_b, "gate_b": gate_b, "w_gate_up": w_gate_up, "w_down": w_down}


def place_rows(route, experts, capacity):
    flat_ids = route.reshape(-1)
    total_rows = flat_ids.shape[0]
    onehot = (flat_ids[:, None] == jnp.arange(experts, dtype=jnp.int32)[None, :]).astype(jnp.int32)
    before = jnp.cumsum(onehot, axis=0) - onehot
    rank_in = jnp.sum(before * onehot, axis=1)
    target = (flat_ids * capacity + rank_in).astype(jnp.int32)
    source = jnp.zeros((experts * capacity,), jnp.int32).at[target].set(jnp.arange(total_rows, dtype=jnp.int32))
    filled = jnp.zeros((experts * capacity,), jnp.int32).at[target].set(1)
    return target, source, filled


def pick_rows(tokens, source, filled, top_count):
    return jnp.where(filled[:, None] > 0, tokens[source // top_count], 0)


def scaled_rows(cotangent, gates, source, filled, top_count):
    weight_of = jnp.where(filled > 0, gates.reshape(-1)[source], 0.0)
    return (cotangent[source // top_count].astype(jnp.float32) * weight_of[:, None]).astype(jnp.bfloat16)


def take_rows(rows, target):
    return rows[target]


def expert_forward(rows, w_gu, w_dn):
    half_width = w_dn.shape[1]
    projected = jnp.dot(rows, w_gu, preferred_element_type=jnp.float32)
    gate_part = projected[:, :half_width]
    up_part = projected[:, half_width:]
    hidden = (gate_part * jax.nn.sigmoid(gate_part) * up_part).astype(jnp.bfloat16)
    produced = lax.dot_general(hidden, w_dn, (((1,), (1,)), ((), ())), preferred_element_type=jnp.float32)
    return produced.astype(jnp.bfloat16)


def expert_backward(rows_in, rows_scaled, w_gu, w_dn):
    half_width = w_dn.shape[1]
    projected = jnp.dot(rows_in, w_gu, preferred_element_type=jnp.float32)
    gate_part = projected[:, :half_width]
    up_part = projected[:, half_width:]
    sigmoid_g = jax.nn.sigmoid(gate_part)
    active = gate_part * sigmoid_g
    hidden = (active * up_part).astype(jnp.bfloat16)
    hidden_grad = jnp.dot(rows_scaled, w_dn, preferred_element_type=jnp.float32)
    gate_grad = hidden_grad * up_part * sigmoid_g * (1.0 + gate_part * (1.0 - sigmoid_g))
    up_grad = hidden_grad * active
    both_grad = jnp.concatenate([gate_grad, up_grad], axis=1).astype(jnp.bfloat16)
    row_grads = lax.dot_general(both_grad, w_gu, (((1,), (1,)), ((), ())), preferred_element_type=jnp.float32)
    return row_grads.astype(jnp.bfloat16), both_grad, hidden


def reference(tokens_a, cotangent_a, route_a, gate_a, tokens_b, route_b, gate_b, w_gate_up, w_down):
    def blocks(array):
        split = array.reshape((N_EXPERT, N_DP, TOK_DEV) + array.shape[1:])
        return jnp.swapaxes(split, 0, 1)

    def to_expert(array):
        return jnp.swapaxes(array.reshape(N_EXPERT, EXPERTS, CAP, D), 0, 1).reshape(EXPERTS, N_EXPERT * CAP, D)

    def to_source(array):
        return jnp.swapaxes(array.reshape(EXPERTS, N_EXPERT, CAP, D), 0, 1).reshape(N_EXPERT, EXPERTS * CAP, D)

    def expert_step(operands):
        w_gu, w_dn, rows_b, rows_in, rows_scaled = operands
        produced = expert_forward(rows_b, w_gu, w_dn)
        row_grads, both_grad, hidden = expert_backward(rows_in, rows_scaled, w_gu, w_dn)
        first = lax.dot_general(rows_in, both_grad, (((0,), (0,)), ((), ())), preferred_element_type=jnp.float32)
        second = lax.dot_general(rows_scaled, hidden, (((0,), (0,)), ((), ())), preferred_element_type=jnp.float32)
        partial_grad = jnp.concatenate([first, second], axis=1).astype(jnp.bfloat16)
        return produced, row_grads, partial_grad

    placing = jax.vmap(partial(place_rows, experts=EXPERTS, capacity=CAP))
    picking = jax.vmap(partial(pick_rows, top_count=TOP))
    scaling = jax.vmap(partial(scaled_rows, top_count=TOP))
    taking = jax.vmap(take_rows)

    def replica(carry, item):
        block_tokens_a, block_cot_a, block_route_a, block_gate_a, block_tokens_b, block_route_b, block_gate_b = item
        target_a, source_a, filled_a = placing(block_route_a)
        target_b, source_b, filled_b = placing(block_route_b)
        send_in = picking(block_tokens_a, source_a, filled_a)
        send_scaled = scaling(block_cot_a, block_gate_a, source_a, filled_a)
        send_b = picking(block_tokens_b, source_b, filled_b)
        produced, row_grads, partial_grad = lax.map(expert_step, (w_gate_up, w_down, to_expert(send_b), to_expert(send_in), to_expert(send_scaled)))
        picked_a = taking(to_source(row_grads), target_a).reshape(N_EXPERT, TOK_DEV, TOP, D).astype(jnp.float32)
        input_grad = jnp.sum(picked_a, axis=2).astype(jnp.bfloat16)
        picked_b = taking(to_source(produced), target_b).reshape(N_EXPERT, TOK_DEV, TOP, D).astype(jnp.float32)
        mixed = jnp.sum(picked_b * block_gate_b[:, :, :, None], axis=2).astype(jnp.bfloat16)
        return carry + partial_grad.astype(jnp.float32), (input_grad, mixed)

    items = tuple(blocks(array) for array in (tokens_a, cotangent_a, route_a, gate_a, tokens_b, route_b, gate_b))
    initial = jnp.zeros((EXPERTS, D, 3 * FF), jnp.float32)
    grads, (input_grad, mixed) = lax.scan(replica, initial, items)
    input_grad = jnp.swapaxes(input_grad, 0, 1).reshape(TOKENS, D)
    mixed = jnp.swapaxes(mixed, 0, 1).reshape(TOKENS, D)
    return input_grad, mixed, grads[:, :, :2 * FF], grads[:, :, 2 * FF:]
```

```python
import functools

import jax
import jax.numpy as jnp
from jax import lax
from jax.experimental import pallas as pl
from jax.experimental.pallas import tpu as pltpu
from jax.sharding import Mesh, PartitionSpec as P

AXES = ("x", "zl", "c", "zh", "y")
SIZES = (4, 4, 2, 2, 4)
BF = jnp.bfloat16
F32 = jnp.float32
PAD = 128
CAP = 20
WIN = 4
BLK = WIN * CAP
VMEM_LIMIT = 50 * 1024 * 1024


def shift_x(value, k, back=False):
    perm = []
    for x in range(4):
        for c in range(2):
            s = (1 if c == 0 else -1) * (-1 if back else 1)
            perm.append((x * 2 + c, ((x + s * k) % 4) * 2 + c))
    return lax.ppermute(value, ("x", "c"), perm)


def shift_z(value, k, back=False):
    step = -1 if k == 3 else k
    perm = []
    for z in range(8):
        for c in range(2):
            s = (1 if c == 0 else -1) * (-1 if back else 1)
            to = (z + s * step) % 8
            perm.append((((z % 4) * 2 + c) * 2 + z // 4, ((to % 4) * 2 + c) * 2 + to // 4))
    return lax.ppermute(value, ("zl", "c", "zh"), perm)


def shift_y(value, k):
    perm = []
    for c in range(2):
        for y in range(4):
            s = 1 if c == 0 else -1
            perm.append((c * 4 + y, c * 4 + (y + s * k) % 4))
    return lax.ppermute(value, ("c", "y"), perm)


def swap_core(value):
    return lax.ppermute(value, "c", [(0, 1), (1, 0)])


def swap_zh(value):
    return lax.ppermute(value, "zh", [(0, 1), (1, 0)])


def call(kernel, out_shape, flops, operands, scratch=(), smem=0):
    nbytes = sum(o.size * o.dtype.itemsize for o in operands)
    nbytes += sum(o.size * o.dtype.itemsize for o in jax.tree.leaves(out_shape))
    specs = [pl.BlockSpec(memory_space=pltpu.SMEM)] * smem
    specs += [pl.BlockSpec(memory_space=pltpu.VMEM)] * (len(operands) - smem)
    return pl.pallas_call(
        kernel,
        out_shape=out_shape,
        in_specs=specs,
        out_specs=jax.tree.map(lambda _: pl.BlockSpec(memory_space=pltpu.VMEM), out_shape),
        scratch_shapes=list(scratch),
        compiler_params=pltpu.CompilerParams(vmem_limit_bytes=VMEM_LIMIT),
        cost_estimate=pl.CostEstimate(flops=flops, bytes_accessed=nbytes, transcendentals=0),
    )(*operands)


def sds(shape, dtype=BF):
    return jax.ShapeDtypeStruct(shape, dtype)


def pack_kernel(route_a, gate_a, route_b, gate_b, tok_a, cot_a, tok_b, out_a, out_c, out_b):
    rows, width = tok_a.shape

    def coded(route, gate):
        lane = lax.broadcasted_iota(jnp.int32, (rows, PAD), 1)
        expert = lane & 31
        value = jnp.zeros((rows, PAD), F32)
        mask = jnp.zeros((rows, PAD), F32)
        for k in range(route.shape[1]):
            hit = route[:, k : k + 1] == expert
            value = jnp.where(hit, gate[:, k : k + 1], value)
            mask = jnp.where(hit, 1.0, mask)
        first = value.astype(BF).astype(F32)
        second = (value - first).astype(BF).astype(F32)
        third = value - first - second
        coded_value = jnp.where(lane < 32, first, jnp.where(lane < 64, second, third))
        return jnp.where(lane < 96, coded_value, mask).astype(BF)

    code_a = coded(route_a[...], gate_a[...])
    code_b = coded(route_b[...], gate_b[...])
    for source, code, out in ((tok_a, code_a, out_a), (cot_a, code_a, out_c), (tok_b, code_b, out_b)):
        out[:, :width] = source[...]
        out[:, width:] = code


def dispatch_kernel(scaled, gated, ids, p0, p1, p2, p3, r0, r1, r2, r3, *rest):
    weights, toks = rest[:-1], rest[-1]
    rows = p0.shape[0]
    width = p0.shape[1] - PAD
    n = WIN * rows
    blocks = (p0, p1, p2, p3)
    for w, block in enumerate(blocks):
        toks[w * rows : (w + 1) * rows, :] = block[:, :width]
    code = jnp.concatenate([block[:, width:] for block in blocks], axis=0)
    sub = lax.broadcasted_iota(jnp.int32, (16, PAD), 0)
    lane = lax.broadcasted_iota(jnp.int32, (16, PAD), 1)
    wanted = jnp.full((16, PAD), -1, jnp.int32)
    for j in range(8):
        wanted = jnp.where(sub == j, ids[j], wanted)
    hit = (lane & 31) == wanted
    nt = (((1,), (1,)), ((), ()))
    pick_gate = jnp.where(hit & (lane < 96), 1.0, 0.0).astype(BF)
    pick_mask = jnp.where(hit & (lane >= 96), 1.0, 0.0).astype(BF)
    gate = lax.dot_general(pick_gate, code, nt, preferred_element_type=F32)
    mask = lax.dot_general(pick_mask, code, nt, preferred_element_type=F32)
    ahead = lax.broadcasted_iota(jnp.int32, (n, n), 0)
    here = lax.broadcasted_iota(jnp.int32, (n, n), 1)
    before = jnp.where((ahead < here) & (ahead // rows == here // rows), 1.0, 0.0).astype(BF)
    rank = jnp.dot(mask.astype(BF), before, preferred_element_type=F32)
    column = lax.broadcasted_iota(jnp.int32, (16, n), 1)
    other = lax.broadcasted_iota(jnp.int32, (16, n), 0) & 1
    slot = rank.astype(jnp.int32) + (column // rows) * CAP + other * BLK
    slot = jnp.where(mask > 0.5, slot, -1)
    place = lax.broadcasted_iota(jnp.int32, (2 * BLK, n), 0)
    for k, out in enumerate((r0, r1, r2, r3)):
        near = place == slot[2 * k : 2 * k + 1, :]
        far = place == slot[2 * k + 1 : 2 * k + 2, :]
        choice = jnp.where(near | far, 1.0, 0.0).astype(BF)
        if scaled or gated:
            gates = jnp.where(near, gate[2 * k : 2 * k + 1, :], 0.0)
            gates = jnp.where(far, gate[2 * k + 1 : 2 * k + 2, :], gates)
        if gated:
            high = gates.astype(BF)
            weights[0][k] = high
            weights[1][k] = (gates - high.astype(F32)).astype(BF)
        elif weights:
            weights[0][k] = choice
        picked = jnp.dot(choice, toks[...], preferred_element_type=F32)
        if scaled:
            picked = picked * jnp.sum(gates, axis=1, keepdims=True)
        out[...] = picked.astype(BF)


def dispatch(ids, blocks, kind):
    rows, padded = blocks[0].shape
    width = padded - PAD
    n = WIN * rows
    out = [sds((2 * BLK, width))] * 4
    keep = {"plain": 1, "scaled": 0, "gated": 2}[kind]
    out += [sds((4, 2 * BLK, n))] * keep
    flops = 2 * 8 * BLK * n * width
    res = call(
        functools.partial(dispatch_kernel, kind == "scaled", kind == "gated"),
        tuple(out), flops, (ids, *blocks), [pltpu.VMEM((n, width), BF)], smem=1,
    )
    return res[:4], res[4:]


def combine_kernel(n_weights, *refs):
    weights = refs[:n_weights]
    own, exchanged, r1, r2, r3 = refs[n_weights : n_weights + 5]
    outs = refs[n_weights + 5 :]
    rows, width = outs[0].shape
    tn = (((0,), (0,)), ((), ()))
    step = min(width, 512)

    @pl.loop(0, width // step)
    def _(i):
        cols = pl.ds(pl.multiple_of(i * step, step), step)
        total = None
        for w in weights:
            for k in range(4):
                if k == 0:
                    values = jnp.concatenate([own[:BLK, cols], exchanged[:BLK, cols]], axis=0)
                else:
                    values = (r1, r2, r3)[k - 1][:, cols]
                part = lax.dot_general(w[k], values, tn, preferred_element_type=F32)
                total = part if total is None else total + part
        total = total.astype(BF)
        for w, out in enumerate(outs):
            out[:, cols] = total[w * rows : (w + 1) * rows, :]


def combine(weights, own, exchanged, returned, rows):
    width = own.shape[1]
    flops = len(weights) * 2 * 8 * BLK * WIN * rows * width
    return call(
        functools.partial(combine_kernel, len(weights)),
        tuple([sds((rows, width))] * 4), flops, (*weights, own, exchanged, *returned),
    )


def expert_a_kernel(a0, a1, a2, a3, ao, c0, c1, c2, c3, co, perm, w_gu, w_dn, rows_in, rows_scaled, both, hidden, cots):
    half = 4 * BLK
    width = a0.shape[1]
    ff = w_dn.shape[1]
    for k, (a, c) in enumerate(((a0, c0), (a1, c1), (a2, c2), (a3, c3))):
        rows_in[k * BLK : (k + 1) * BLK, :] = a[:BLK, :]
        cots[k * BLK : (k + 1) * BLK, :] = c[:BLK, :]
    rows_in[half:, :] = ao[...]
    cots[half:, :] = co[...]
    wide = min(512, width)

    @pl.loop(0, width // wide)
    def _(i):
        cols = pl.ds(pl.multiple_of(i * wide, wide), wide)
        for h in range(2):
            rs = slice(h * half, (h + 1) * half)
            rows_scaled[rs, cols] = jnp.dot(perm[...], cots[rs, cols], preferred_element_type=F32).astype(BF)

    step = min(256, ff)

    @pl.loop(0, ff // step)
    def _(i):
        gc = pl.ds(pl.multiple_of(i * step, step), step)
        uc = pl.ds(pl.multiple_of(ff + i * step, step), step)
        for h in range(2):
            rs = slice(h * half, (h + 1) * half)
            g = jnp.dot(rows_in[rs, :], w_gu[:, gc], preferred_element_type=F32)
            u = jnp.dot(rows_in[rs, :], w_gu[:, uc], preferred_element_type=F32)
            grad = jnp.dot(rows_scaled[rs, :], w_dn[:, gc], preferred_element_type=F32)
            s = jax.nn.sigmoid(g)
            active = g * s
            hidden[rs, gc] = (active * u).astype(BF)
            both[rs, gc] = (grad * u * s * (1.0 + g * (1.0 - s))).astype(BF)
            both[rs, uc] = (grad * active).astype(BF)


def row_grad_kernel(both, w_gu, own, other):
    half = 4 * BLK
    width = w_gu.shape[0]
    step = min(256, width)
    nt = (((1,), (1,)), ((), ()))

    @pl.loop(0, width // step)
    def _(i):
        cols = pl.ds(pl.multiple_of(i * step, step), step)
        for h, out in enumerate((own, other)):
            rs = slice(h * half, (h + 1) * half)
            out[:, cols] = lax.dot_general(both[rs, :], w_gu[cols, :], nt, preferred_element_type=F32).astype(BF)


def grad_kernel(chunk_ids, rows_in, rows_scaled, both, hidden, g0, g1, g2, g3):
    deep = g0.shape[0]
    wide = both.shape[1]
    tn = (((0,), (0,)), ((), ()))
    for j, out in enumerate((g0, g1, g2, g3)):
        cols = pl.ds(pl.multiple_of(chunk_ids[j] * deep, deep), deep)
        out[:, :wide] = lax.dot_general(rows_in[:, cols], both[...], tn, preferred_element_type=F32).astype(BF)
        out[:, wide:] = lax.dot_general(rows_scaled[:, cols], hidden[...], tn, preferred_element_type=F32).astype(BF)


def expert_b_kernel(b0, b1, b2, b3, bo, w_gu, w_dn, own, other, rows_in, hidden):
    half = 4 * BLK
    width = b0.shape[1]
    ff = w_dn.shape[1]
    for k, b in enumerate((b0, b1, b2, b3)):
        rows_in[k * BLK : (k + 1) * BLK, :] = b[:BLK, :]
    rows_in[half:, :] = bo[...]
    step = min(256, ff)

    @pl.loop(0, ff // step)
    def _(i):
        gc = pl.ds(pl.multiple_of(i * step, step), step)
        uc = pl.ds(pl.multiple_of(ff + i * step, step), step)
        for h in range(2):
            rs = slice(h * half, (h + 1) * half)
            g = jnp.dot(rows_in[rs, :], w_gu[:, gc], preferred_element_type=F32)
            u = jnp.dot(rows_in[rs, :], w_gu[:, uc], preferred_element_type=F32)
            hidden[rs, gc] = (g * jax.nn.sigmoid(g) * u).astype(BF)

    nt = (((1,), (1,)), ((), ()))
    wide = min(256, width)

    @pl.loop(0, width // wide)
    def _(i):
        cols = pl.ds(pl.multiple_of(i * wide, wide), wide)
        for h, out in enumerate((own, other)):
            rs = slice(h * half, (h + 1) * half)
            out[:, cols] = lax.dot_general(hidden[rs, :], w_dn[cols, :], nt, preferred_element_type=F32).astype(BF)


def gather_window(shift, payload):
    return (payload, shift(payload, 1), shift(payload, 2), shift(payload, 3))


def send_rows(shift, rows):
    got = (rows[0], shift(rows[1], 1), shift(rows[2], 2), shift(rows[3], 3))
    other = swap_core(jnp.concatenate([r[BLK:] for r in got], axis=0))
    return got, other


def return_rows(shift, own, other):
    exchanged = swap_core(other)
    back = []
    for k in (1, 2, 3):
        rs = slice(k * BLK, (k + 1) * BLK)
        back.append(shift(jnp.concatenate([own[rs], exchanged[rs]], axis=0), k, True))
    return exchanged, back


def return_window(shift, parts):
    total = parts[0].astype(F32)
    for k in (1, 2, 3):
        total = total + shift(parts[k], k, True).astype(F32)
    return total.astype(BF)


def reduce_y(chunks):
    relayed = shift_y(chunks[2], 1)
    direct = shift_y(chunks[3], 3)
    summed = shift_y((chunks[1].astype(F32) + relayed.astype(F32)).astype(BF), 1)
    return chunks[0].astype(F32) + direct.astype(F32) + summed.astype(F32)


def body(tokens_a, cotangent_a, route_a, gate_a, tokens_b, route_b, gate_b, w_gate_up, w_down):
    rows, width = tokens_a.shape
    w_gu, w_dn = w_gate_up[0], w_down[0]
    ff = w_dn.shape[1]
    x, zl, c = lax.axis_index("x"), lax.axis_index("zl"), lax.axis_index("c")
    zh, y = lax.axis_index("zh"), lax.axis_index("y")
    s = 1 - 2 * c
    k8 = jnp.arange(8, dtype=jnp.int32) // 2
    c8 = c ^ (jnp.arange(8, dtype=jnp.int32) & 1)
    ids_x = (((x + s * k8) & 3) * 4 + zl) * 2 + c8
    ids_z = (x * 4 + ((zl + s * k8) & 3)) * 2 + c8
    k4 = (y + s * jnp.arange(4, dtype=jnp.int32)) & 3
    chunks_far = (1 - zh) * 4 + k4
    chunks_near = zh * 4 + k4

    padded = sds((rows, width + PAD))
    pay_a, pay_c, pay_b = call(
        pack_kernel, (padded, padded, padded), 0,
        (route_a, gate_a, route_b, gate_b, tokens_a, cotangent_a, tokens_b),
    )
    rows_a, keep_a = dispatch(ids_x, gather_window(shift_z, pay_a), "plain")
    rows_c, _ = dispatch(ids_z, gather_window(shift_x, pay_c), "scaled")
    got_a, other_a = send_rows(shift_x, rows_a)
    got_c, other_c = send_rows(shift_z, rows_c)
    rows_b, keep_b = dispatch(ids_x, gather_window(shift_z, pay_b), "gated")
    got_b, other_b = send_rows(shift_x, rows_b)

    half = 4 * BLK
    i = jnp.arange(half, dtype=jnp.int32)
    source = ((i % BLK) // CAP) * BLK + (i // BLK) * CAP + i % CAP
    perm = (source[:, None] == i[None, :]).astype(BF)
    rows_in, rows_scaled, both, hidden = call(
        expert_a_kernel,
        (sds((2 * half, width)), sds((2 * half, width)), sds((2 * half, 2 * ff)), sds((2 * half, ff))),
        2 * 2 * half * width * 3 * ff,
        (*got_a, other_a, *got_c, other_c, perm, w_gu, w_dn),
        [pltpu.VMEM((2 * half, width), BF)],
    )
    chunk = sds((width // 8, 3 * ff))
    grad_flops = 2 * 2 * half * width // 2 * 3 * ff
    operands = (rows_in, rows_scaled, both, hidden)
    far = call(grad_kernel, (chunk,) * 4, grad_flops, (chunks_far, *operands), smem=1)
    own_a, back_a = call(
        row_grad_kernel, (sds((half, width)),) * 2, 2 * 2 * half * width * 2 * ff, (both, w_gu)
    )
    near = call(grad_kernel, (chunk,) * 4, grad_flops, (chunks_near, *operands), smem=1)
    far_total = swap_zh(reduce_y(far).astype(BF))
    near_total = reduce_y(near)

    exchanged_a, returned_a = return_rows(shift_x, own_a, back_a)
    own_b, back_b = call(
        expert_b_kernel, (sds((half, width)),) * 2, 2 * 2 * half * width * 3 * ff,
        (*got_b, other_b, w_gu, w_dn),
        [pltpu.VMEM((2 * half, width), BF), pltpu.VMEM((2 * half, ff), BF)],
    )
    exchanged_b, returned_b = return_rows(shift_x, own_b, back_b)
    input_grad = return_window(shift_z, combine(keep_a, own_a, exchanged_a, returned_a, rows))
    mixed = return_window(shift_z, combine(keep_b, own_b, exchanged_b, returned_b, rows))
    grads = near_total + far_total.astype(F32)
    return (input_grad, mixed, grads[None, :, : 2 * ff], grads[None, :, 2 * ff :])


def solution(mesh):
    fine = Mesh(mesh.devices.reshape(SIZES), AXES)
    tokens = P(AXES, None)
    return jax.shard_map(
        body,
        mesh=fine,
        in_specs=(tokens,) * 7 + (P(("x", "zl", "c"), None, None),) * 2,
        out_specs=(tokens, tokens) + (P(("x", "zl", "c"), ("zh", "y"), None),) * 2,
        check_vma=False,
    )
```

```python
import functools

import jax
import jax.numpy as jnp
from jax import lax
from jax.experimental import pallas as pl
from jax.experimental.pallas import tpu as pltpu
from jax.sharding import Mesh, PartitionSpec as P

AXES = ("x", "zl", "c", "zh", "y")
SIZES = (4, 4, 2, 2, 4)
BF = jnp.bfloat16
F32 = jnp.float32
PAD = 128
CAP = 20
WIN = 4
BLK = WIN * CAP
KEEP = {"plain": 1, "scaled": 0, "gated": 2}
MIB = 1024 * 1024


def shift_x(value, k, back=False):
    perm = []
    for x in range(4):
        for c in range(2):
            s = (1 if c == 0 else -1) * (-1 if back else 1)
            perm.append((x * 2 + c, ((x + s * k) % 4) * 2 + c))
    return lax.ppermute(value, ("x", "c"), perm)


def shift_z(value, k, back=False):
    step = -1 if k == 3 else k
    perm = []
    for z in range(8):
        for c in range(2):
            s = (1 if c == 0 else -1) * (-1 if back else 1)
            to = (z + s * step) % 8
            perm.append((((z % 4) * 2 + c) * 2 + z // 4, ((to % 4) * 2 + c) * 2 + to // 4))
    return lax.ppermute(value, ("zl", "c", "zh"), perm)


def shift_y(value, k):
    perm = []
    for c in range(2):
        for y in range(4):
            s = 1 if c == 0 else -1
            perm.append((c * 4 + y, c * 4 + (y + s * k) % 4))
    return lax.ppermute(value, ("c", "y"), perm)


def swap_core(value):
    return lax.ppermute(value, "c", [(0, 1), (1, 0)])


def swap_zh(value):
    return lax.ppermute(value, "zh", [(0, 1), (1, 0)])


def call(kernel, out_shape, flops, operands, scratch=(), smem=0, mib=10):
    nbytes = sum(o.size * o.dtype.itemsize for o in operands)
    nbytes += sum(o.size * o.dtype.itemsize for o in jax.tree.leaves(out_shape))
    vmem = pl.BlockSpec(memory_space=pltpu.VMEM)
    specs = [pl.BlockSpec(memory_space=pltpu.SMEM)] * smem
    specs += [vmem] * (len(operands) - smem)
    return pl.pallas_call(
        kernel,
        out_shape=out_shape,
        in_specs=specs,
        out_specs=jax.tree.map(lambda _: vmem, out_shape),
        scratch_shapes=list(scratch),
        compiler_params=pltpu.CompilerParams(vmem_limit_bytes=mib * MIB),
        cost_estimate=pl.CostEstimate(flops=flops, bytes_accessed=nbytes, transcendentals=0),
    )(*operands)


def after(value, *others):
    return lax.optimization_barrier((value, *others))[0]


def sds(shape, dtype=BF):
    return jax.ShapeDtypeStruct(shape, dtype)


def code_kernel(stacked, code_a, code_b):
    top = stacked.shape[0] // 4
    rows = stacked.shape[1]
    sub = lax.broadcasted_iota(jnp.int32, (PAD, rows), 0)
    expert = (sub & 31).astype(F32)
    for at, out in ((0, code_a), (2 * top, code_b)):
        value = jnp.zeros((PAD, rows), F32)
        mask = jnp.zeros((PAD, rows), F32)
        for k in range(at, at + top):
            hit = stacked[k : k + 1, :] == expert
            value = jnp.where(hit, stacked[k + top : k + top + 1, :], value)
            mask = jnp.where(hit, 1.0, mask)
        first = value.astype(BF).astype(F32)
        second = (value - first).astype(BF).astype(F32)
        third = value - first - second
        coded = jnp.where(sub < 32, first, jnp.where(sub < 64, second, third))
        out[...] = jnp.where(sub < 96, coded, mask).T.astype(BF)


def dispatch_kernel(jobs, *refs):
    n = len(jobs)
    ids, refs = refs[:n], refs[n:]
    windows = 1 + max(window for _, window, _ in jobs)
    blocks, outs, toks = refs[: WIN * windows], refs[WIN * windows : -1], refs[-1]
    for j, (kind, window, at) in enumerate(jobs):
        keep = KEEP[kind]
        near = blocks[WIN * window : WIN * window + WIN]
        pick_rows(kind, ids[j], near, at * (toks.shape[1] + PAD), outs[:4], outs[4 : 4 + keep], toks)
        outs = outs[4 + keep :]


def pick_rows(kind, ids, blocks, start, outs, weights, toks):
    scaled, gated = kind == "scaled", kind == "gated"
    rows, width = blocks[0].shape[0], toks.shape[1]
    stop = start + width
    n = WIN * rows
    for w, block in enumerate(blocks):
        toks[w * rows : (w + 1) * rows, :] = block[:, start:stop]
    code = jnp.concatenate([block[:, stop : stop + PAD] for block in blocks], axis=0)
    sub = lax.broadcasted_iota(jnp.int32, (16, PAD), 0)
    lane = lax.broadcasted_iota(jnp.int32, (16, PAD), 1)
    wanted = jnp.full((16, PAD), -1, jnp.int32)
    for j in range(8):
        wanted = jnp.where(sub == j, ids[j], wanted)
    hit = (lane & 31) == wanted
    nt = (((1,), (1,)), ((), ()))
    pick_gate = jnp.where(hit & (lane < 96), 1.0, 0.0).astype(BF)
    pick_mask = jnp.where(hit & (lane >= 96), 1.0, 0.0).astype(BF)
    gate = lax.dot_general(pick_gate, code, nt, preferred_element_type=F32)
    mask = lax.dot_general(pick_mask, code, nt, preferred_element_type=F32)
    ahead = lax.broadcasted_iota(jnp.int32, (n, n), 0)
    here = lax.broadcasted_iota(jnp.int32, (n, n), 1)
    before = jnp.where((ahead < here) & (ahead // rows == here // rows), 1.0, 0.0).astype(BF)
    rank = jnp.dot(mask.astype(BF), before, preferred_element_type=F32)
    column = lax.broadcasted_iota(jnp.int32, (16, n), 1)
    other = lax.broadcasted_iota(jnp.int32, (16, n), 0) & 1
    slot = rank.astype(jnp.int32) + (column // rows) * CAP + other * BLK
    slot = jnp.where(mask > 0.5, slot, -1)
    place = lax.broadcasted_iota(jnp.int32, (2 * BLK, n), 0)
    for k, out in enumerate(outs):
        near = place == slot[2 * k : 2 * k + 1, :]
        far = place == slot[2 * k + 1 : 2 * k + 2, :]
        choice = jnp.where(near | far, 1.0, 0.0).astype(BF)
        if scaled or gated:
            gates = jnp.where(near, gate[2 * k : 2 * k + 1, :], 0.0)
            gates = jnp.where(far, gate[2 * k + 1 : 2 * k + 2, :], gates)
        if gated:
            high = gates.astype(BF)
            weights[0][k] = high
            weights[1][k] = (gates - high.astype(F32)).astype(BF)
        elif weights:
            weights[0][k] = choice
        picked = jnp.dot(choice, toks[...], preferred_element_type=F32)
        if scaled:
            picked = picked * jnp.sum(gates, axis=1, keepdims=True)
        out[...] = picked.astype(BF)


def dispatch(ids, windows, jobs, width):
    n = WIN * windows[0][0].shape[0]
    out, counts = [], []
    for kind, _, _ in jobs:
        out += [sds((2 * BLK, width))] * 4 + [sds((4, 2 * BLK, n))] * KEEP[kind]
        counts.append(4 + KEEP[kind])
    flops = 2 * 8 * BLK * n * width * len(jobs)
    blocks = [block for window in windows for block in window]
    res = call(
        functools.partial(dispatch_kernel, jobs), tuple(out), flops,
        (*ids, *blocks), [pltpu.VMEM((n, width), BF)], smem=len(jobs), mib=8,
    )
    parts = []
    for count in counts:
        parts.append((res[:4], res[4:count]))
        res = res[count:]
    return parts


def combine_kernel(n_weights, *refs):
    weights = refs[:n_weights]
    own, exchanged, r1, r2, r3 = refs[n_weights : n_weights + 5]
    outs = refs[n_weights + 5 :]
    rows, width = outs[0].shape
    tn = (((0,), (0,)), ((), ()))
    step = min(width, 512)

    @pl.loop(0, width // step)
    def _(i):
        cols = pl.ds(pl.multiple_of(i * step, step), step)
        total = None
        for w in weights:
            for k in range(4):
                if k == 0:
                    values = jnp.concatenate([own[:BLK, cols], exchanged[:BLK, cols]], axis=0)
                else:
                    values = (r1, r2, r3)[k - 1][:, cols]
                part = lax.dot_general(w[k], values, tn, preferred_element_type=F32)
                total = part if total is None else total + part
        total = total.astype(BF)
        for w, out in enumerate(outs):
            out[:, cols] = total[w * rows : (w + 1) * rows, :]


def combine(weights, own, exchanged, returned, rows):
    width = own.shape[1]
    flops = len(weights) * 2 * 8 * BLK * WIN * rows * width
    return call(
        functools.partial(combine_kernel, len(weights)),
        tuple([sds((rows, width))] * 4), flops, (*weights, own, exchanged, *returned),
    )


def expert_a_kernel(a0, a1, a2, a3, ao, c0, c1, c2, c3, co, perm, w_gu, w_dn, rows_in, rows_scaled, both, hidden, cots):
    half = 4 * BLK
    width = a0.shape[1]
    ff = w_dn.shape[1]
    for k, (a, c) in enumerate(((a0, c0), (a1, c1), (a2, c2), (a3, c3))):
        rows_in[k * BLK : (k + 1) * BLK, :] = a[:BLK, :]
        cots[k * BLK : (k + 1) * BLK, :] = c[:BLK, :]
    rows_in[half:, :] = ao[...]
    cots[half:, :] = co[...]
    wide = min(512, width)

    @pl.loop(0, width // wide)
    def _(i):
        cols = pl.ds(pl.multiple_of(i * wide, wide), wide)
        for h in range(2):
            rs = slice(h * half, (h + 1) * half)
            rows_scaled[rs, cols] = jnp.dot(perm[...], cots[rs, cols], preferred_element_type=F32).astype(BF)

    step = min(256, ff)

    @pl.loop(0, ff // step)
    def _(i):
        gc = pl.ds(pl.multiple_of(i * step, step), step)
        uc = pl.ds(pl.multiple_of(ff + i * step, step), step)
        g = jnp.dot(rows_in[...], w_gu[:, gc], preferred_element_type=F32)
        u = jnp.dot(rows_in[...], w_gu[:, uc], preferred_element_type=F32)
        grad = jnp.dot(rows_scaled[...], w_dn[:, gc], preferred_element_type=F32)
        s = jax.nn.sigmoid(g)
        active = g * s
        hidden[:, gc] = (active * u).astype(BF)
        both[:, gc] = (grad * u * s * (1.0 + g * (1.0 - s))).astype(BF)
        both[:, uc] = (grad * active).astype(BF)


def row_grad_kernel(both, w_gu, own, other):
    half = 4 * BLK
    width = w_gu.shape[0]
    step = min(256, width)
    nt = (((1,), (1,)), ((), ()))

    @pl.loop(0, width // step)
    def _(i):
        cols = pl.ds(pl.multiple_of(i * step, step), step)
        for h, out in enumerate((own, other)):
            rs = slice(h * half, (h + 1) * half)
            out[:, cols] = lax.dot_general(both[rs, :], w_gu[cols, :], nt, preferred_element_type=F32).astype(BF)


def grad_kernel(chunk_ids, rows_in, rows_scaled, both, hidden, g0, g1, g2, g3):
    deep = g0.shape[0]
    wide = both.shape[1]
    tn = (((0,), (0,)), ((), ()))
    for j, out in enumerate((g0, g1, g2, g3)):
        cols = pl.ds(pl.multiple_of(chunk_ids[j] * deep, deep), deep)
        out[:, :wide] = lax.dot_general(rows_in[:, cols], both[...], tn, preferred_element_type=F32).astype(BF)
        out[:, wide:] = lax.dot_general(rows_scaled[:, cols], hidden[...], tn, preferred_element_type=F32).astype(BF)


def expert_b_kernel(b0, b1, b2, b3, bo, w_gu, w_dn, own, other, rows_in, hidden):
    half = 4 * BLK
    width = b0.shape[1]
    ff = w_dn.shape[1]
    for k, b in enumerate((b0, b1, b2, b3)):
        rows_in[k * BLK : (k + 1) * BLK, :] = b[:BLK, :]
    rows_in[half:, :] = bo[...]
    step = min(256, ff)

    @pl.loop(0, ff // step)
    def _(i):
        gc = pl.ds(pl.multiple_of(i * step, step), step)
        uc = pl.ds(pl.multiple_of(ff + i * step, step), step)
        g = jnp.dot(rows_in[...], w_gu[:, gc], preferred_element_type=F32)
        u = jnp.dot(rows_in[...], w_gu[:, uc], preferred_element_type=F32)
        hidden[:, gc] = (g * jax.nn.sigmoid(g) * u).astype(BF)

    nt = (((1,), (1,)), ((), ()))
    wide = min(256, width)

    @pl.loop(0, width // wide)
    def _(i):
        cols = pl.ds(pl.multiple_of(i * wide, wide), wide)
        res = lax.dot_general(hidden[...], w_dn[cols, :], nt, preferred_element_type=F32).astype(BF)
        own[:, cols] = res[:half]
        other[:, cols] = res[half:]


def gather_window(shift, block):
    return (block, shift(block, 1), shift(block, 2), shift(block, 3))


def send_rows(shift, rows, first=None, late=()):
    near = shift(rows[1], 1)
    last = rows[3] if late is None else after(rows[3], near, *late)
    got = (rows[0], near, shift(rows[2], 2), shift(last, 3))
    far = got if first is None else tuple(lax.optimization_barrier((*got, first))[:4])
    other = swap_core(jnp.concatenate([r[BLK:] for r in far], axis=0))
    return got, other


def pair_rows(own, other):
    exchanged = swap_core(other)
    pairs = []
    for k in (1, 2, 3):
        rs = slice(k * BLK, (k + 1) * BLK)
        pairs.append(jnp.concatenate([own[rs], exchanged[rs]], axis=0))
    return exchanged, pairs


def return_rows(shift, pairs):
    near = shift(pairs[0], 1, True)
    return near, shift(pairs[1], 2, True), shift(after(pairs[2], near), 3, True)


def return_window(shift, parts):
    total = parts[0].astype(F32)
    for k in (1, 2, 3):
        total = total + shift(parts[k], k, True).astype(F32)
    return total.astype(BF)


def reduce_y(chunks, first=None):
    relayed = shift_y(chunks[2], 1)
    direct = shift_y(chunks[3] if first is None else after(chunks[3], first), 3)
    summed = shift_y((chunks[1].astype(F32) + relayed.astype(F32)).astype(BF), 1)
    return chunks[0].astype(F32) + direct.astype(F32) + summed.astype(F32), direct, summed


def body(tokens_a, cotangent_a, route_a, gate_a, tokens_b, route_b, gate_b, w_gate_up, w_down):
    rows, width = tokens_a.shape
    w_gu, w_dn = w_gate_up[0], w_down[0]
    ff = w_dn.shape[1]
    x, zl, c = lax.axis_index("x"), lax.axis_index("zl"), lax.axis_index("c")
    zh, y = lax.axis_index("zh"), lax.axis_index("y")
    s = 1 - 2 * c
    k8 = jnp.arange(8, dtype=jnp.int32) // 2
    c8 = c ^ (jnp.arange(8, dtype=jnp.int32) & 1)
    ids_x = (((x + s * k8) & 3) * 4 + zl) * 2 + c8
    ids_z = (x * 4 + ((zl + s * k8) & 3)) * 2 + c8
    k4 = (y + s * jnp.arange(4, dtype=jnp.int32)) & 3
    chunks_far = (1 - zh) * 4 + k4
    chunks_near = zh * 4 + k4

    stacked = jnp.concatenate([route_a.T.astype(F32), gate_a.T, route_b.T.astype(F32), gate_b.T], axis=0)
    code_a, code_b = call(code_kernel, (sds((rows, PAD)),) * 2, 0, (stacked,), mib=2)
    win_ab = gather_window(shift_z, jnp.concatenate([tokens_a, code_a, tokens_b, code_b], axis=1))
    win_c = gather_window(shift_x, jnp.concatenate([cotangent_a, code_a], axis=1))
    (rows_a, keep_a), (rows_c, _), (rows_b, keep_b) = dispatch(
        (ids_x, ids_z, ids_x), (win_ab, win_c), (("plain", 0, 0), ("scaled", 1, 0), ("gated", 0, 1)), width
    )
    got_a, other_a = send_rows(shift_x, rows_a)
    got_c, other_c = send_rows(shift_z, rows_c)

    half = 4 * BLK
    i = jnp.arange(half, dtype=jnp.int32)
    source = ((i % BLK) // CAP) * BLK + (i // BLK) * CAP + i % CAP
    perm = (source[:, None] == i[None, :]).astype(BF)
    rows_in, rows_scaled, both, hidden = call(
        expert_a_kernel,
        (sds((2 * half, width)), sds((2 * half, width)), sds((2 * half, 2 * ff)), sds((2 * half, ff))),
        2 * 2 * half * width * 3 * ff,
        (*got_a, other_a, *got_c, other_c, perm, w_gu, w_dn),
        [pltpu.VMEM((2 * half, width), BF)], mib=9,
    )
    chunk = sds((width // 8, 3 * ff))
    grad_flops = 2 * 2 * half * width // 2 * 3 * ff
    operands = (rows_in, rows_scaled, both, hidden)
    far = call(grad_kernel, (chunk,) * 4, grad_flops, (chunks_far, *operands), smem=1)
    own_a, back_a = call(
        row_grad_kernel, (sds((half, width)),) * 2, 2 * 2 * half * width * 2 * ff, (after(both, far), w_gu)
    )
    got_b, other_b = send_rows(shift_x, after(rows_b, got_a[2]), back_a, None)
    far_sum, direct, summed = reduce_y(far)
    near = call(grad_kernel, (chunk,) * 4, grad_flops, (after(chunks_near, back_a), *operands), smem=1)
    near_total, _, _ = reduce_y(after(near, direct), summed)
    far_total = swap_zh(far_sum.astype(BF))

    exchanged_a, pairs_a = pair_rows(own_a, back_a)
    returned_a = return_rows(shift_x, pairs_a)
    own_b, back_b = call(
        expert_b_kernel, (sds((half, width)),) * 2, 2 * 2 * half * width * 3 * ff,
        (*got_b, after(other_b, near, pairs_a), w_gu, w_dn),
        [pltpu.VMEM((2 * half, width), BF), pltpu.VMEM((2 * half, ff), BF)], mib=9,
    )
    exchanged_b, pairs_b = pair_rows(own_b, back_b)
    returned_b = return_rows(shift_x, after(pairs_b, returned_a[0], returned_a[1]))
    input_grad = return_window(shift_z, combine(keep_a, after(own_a, pairs_b), exchanged_a, returned_a, rows))
    mixed = return_window(shift_z, combine(keep_b, own_b, exchanged_b, returned_b, rows))
    grads = near_total + far_total.astype(F32)
    return (input_grad, mixed, grads[None, :, : 2 * ff], grads[None, :, 2 * ff :])


def solution(mesh):
    fine = Mesh(mesh.devices.reshape(SIZES), AXES)
    tokens = P(AXES, None)
    return jax.shard_map(
        body,
        mesh=fine,
        in_specs=(tokens,) * 7 + (P(("x", "zl", "c"), None, None),) * 2,
        out_specs=(tokens, tokens) + (P(("x", "zl", "c"), ("zh", "y"), None),) * 2,
        check_vma=False,
    )
```

```python
import functools

import jax
import jax.numpy as jnp
from jax import lax
from jax.experimental import pallas as pl
from jax.experimental.pallas import tpu as pltpu
from jax.sharding import Mesh, PartitionSpec as P

AXES = ("x", "zl", "c", "zh", "y")
SIZES = (4, 4, 2, 2, 4)
BF = jnp.bfloat16
F32 = jnp.float32
PAD = 128
CAP = 20
WIN = 4
BLK = WIN * CAP
KEEP = {"plain": 1, "scaled": 0, "gated": 2}
MIB = 1024 * 1024


def shift_x(value, k, back=False):
    perm = []
    for x in range(4):
        for c in range(2):
            s = (1 if c == 0 else -1) * (-1 if back else 1)
            perm.append((x * 2 + c, ((x + s * k) % 4) * 2 + c))
    return lax.ppermute(value, ("x", "c"), perm)


def shift_z(value, k, back=False):
    step = -1 if k == 3 else k
    perm = []
    for z in range(8):
        for c in range(2):
            s = (1 if c == 0 else -1) * (-1 if back else 1)
            to = (z + s * step) % 8
            perm.append((((z % 4) * 2 + c) * 2 + z // 4, ((to % 4) * 2 + c) * 2 + to // 4))
    return lax.ppermute(value, ("zl", "c", "zh"), perm)


def shift_y(value, k):
    perm = []
    for c in range(2):
        for y in range(4):
            s = 1 if c == 0 else -1
            perm.append((c * 4 + y, c * 4 + (y + s * k) % 4))
    return lax.ppermute(value, ("c", "y"), perm)


def swap_core(value):
    return lax.ppermute(value, "c", [(0, 1), (1, 0)])


def swap_zh(value):
    return lax.ppermute(value, "zh", [(0, 1), (1, 0)])


def call(kernel, out_shape, flops, operands, scratch=(), smem=0, mib=10):
    nbytes = sum(o.size * o.dtype.itemsize for o in operands)
    nbytes += sum(o.size * o.dtype.itemsize for o in jax.tree.leaves(out_shape))
    vmem = pl.BlockSpec(memory_space=pltpu.VMEM)
    specs = [pl.BlockSpec(memory_space=pltpu.SMEM)] * smem
    specs += [vmem] * (len(operands) - smem)
    return pl.pallas_call(
        kernel,
        out_shape=out_shape,
        in_specs=specs,
        out_specs=jax.tree.map(lambda _: vmem, out_shape),
        scratch_shapes=list(scratch),
        compiler_params=pltpu.CompilerParams(vmem_limit_bytes=mib * MIB),
        cost_estimate=pl.CostEstimate(flops=flops, bytes_accessed=nbytes, transcendentals=0),
    )(*operands)


def after(value, *others):
    return lax.optimization_barrier((value, *others))[0]


def sds(shape, dtype=BF):
    return jax.ShapeDtypeStruct(shape, dtype)


def code_kernel(stacked, code_a, code_b):
    top = stacked.shape[0] // 4
    rows = stacked.shape[1]
    sub = lax.broadcasted_iota(jnp.int32, (PAD, rows), 0)
    expert = (sub & 31).astype(F32)
    for at, out in ((0, code_a), (2 * top, code_b)):
        value = jnp.zeros((PAD, rows), F32)
        mask = jnp.zeros((PAD, rows), F32)
        for k in range(at, at + top):
            hit = stacked[k : k + 1, :] == expert
            value = jnp.where(hit, stacked[k + top : k + top + 1, :], value)
            mask = jnp.where(hit, 1.0, mask)
        first = value.astype(BF).astype(F32)
        second = (value - first).astype(BF).astype(F32)
        third = value - first - second
        coded = jnp.where(sub < 32, first, jnp.where(sub < 64, second, third))
        out[...] = jnp.where(sub < 96, coded, mask).T.astype(BF)


def dispatch_kernel(jobs, *refs):
    n = len(jobs)
    ids, refs = refs[:n], refs[n:]
    windows = 1 + max(window for _, window, _ in jobs)
    blocks, outs, toks = refs[: WIN * windows], refs[WIN * windows : -1], refs[-1]
    for j, (kind, window, at) in enumerate(jobs):
        keep = KEEP[kind]
        near = blocks[WIN * window : WIN * window + WIN]
        pick_rows(kind, ids[j], near, at * (toks.shape[1] + PAD), outs[:4], outs[4 : 4 + keep], toks)
        outs = outs[4 + keep :]


def pick_rows(kind, ids, blocks, start, outs, weights, toks):
    scaled, gated = kind == "scaled", kind == "gated"
    rows, width = blocks[0].shape[0], toks.shape[1]
    stop = start + width
    n = WIN * rows
    for w, block in enumerate(blocks):
        toks[w * rows : (w + 1) * rows, :] = block[:, start:stop]
    code = jnp.concatenate([block[:, stop : stop + PAD] for block in blocks], axis=0)
    sub = lax.broadcasted_iota(jnp.int32, (16, PAD), 0)
    lane = lax.broadcasted_iota(jnp.int32, (16, PAD), 1)
    wanted = jnp.full((16, PAD), -1, jnp.int32)
    for j in range(8):
        wanted = jnp.where(sub == j, ids[j], wanted)
    hit = (lane & 31) == wanted
    nt = (((1,), (1,)), ((), ()))
    pick_gate = jnp.where(hit & (lane < 96), 1.0, 0.0).astype(BF)
    pick_mask = jnp.where(hit & (lane >= 96), 1.0, 0.0).astype(BF)
    gate = lax.dot_general(pick_gate, code, nt, preferred_element_type=F32)
    mask = lax.dot_general(pick_mask, code, nt, preferred_element_type=F32)
    ahead = lax.broadcasted_iota(jnp.int32, (n, n), 0)
    here = lax.broadcasted_iota(jnp.int32, (n, n), 1)
    before = jnp.where((ahead < here) & (ahead // rows == here // rows), 1.0, 0.0).astype(BF)
    rank = jnp.dot(mask.astype(BF), before, preferred_element_type=F32)
    column = lax.broadcasted_iota(jnp.int32, (16, n), 1)
    other = lax.broadcasted_iota(jnp.int32, (16, n), 0) & 1
    slot = rank.astype(jnp.int32) + (column // rows) * CAP + other * BLK
    slot = jnp.where(mask > 0.5, slot, -1)
    place = lax.broadcasted_iota(jnp.int32, (2 * BLK, n), 0)
    for k, out in enumerate(outs):
        near = place == slot[2 * k : 2 * k + 1, :]
        far = place == slot[2 * k + 1 : 2 * k + 2, :]
        choice = jnp.where(near | far, 1.0, 0.0).astype(BF)
        if scaled or gated:
            gates = jnp.where(near, gate[2 * k : 2 * k + 1, :], 0.0)
            gates = jnp.where(far, gate[2 * k + 1 : 2 * k + 2, :], gates)
        if gated:
            high = gates.astype(BF)
            weights[0][k] = high
            weights[1][k] = (gates - high.astype(F32)).astype(BF)
        elif weights:
            weights[0][k] = choice
        picked = jnp.dot(choice, toks[...], preferred_element_type=F32)
        if scaled:
            picked = picked * jnp.sum(gates, axis=1, keepdims=True)
        out[...] = picked.astype(BF)


def dispatch(ids, windows, jobs, width):
    n = WIN * windows[0][0].shape[0]
    out, counts = [], []
    for kind, _, _ in jobs:
        out += [sds((2 * BLK, width))] * 4 + [sds((4, 2 * BLK, n))] * KEEP[kind]
        counts.append(4 + KEEP[kind])
    flops = 2 * 8 * BLK * n * width * len(jobs)
    blocks = [block for window in windows for block in window]
    res = call(
        functools.partial(dispatch_kernel, jobs), tuple(out), flops,
        (*ids, *blocks), [pltpu.VMEM((n, width), BF)], smem=len(jobs), mib=8,
    )
    parts = []
    for count in counts:
        parts.append((res[:4], res[4:count]))
        res = res[count:]
    return parts


def combine_kernel(n_weights, *refs):
    weights = refs[:n_weights]
    own, exchanged, r1, r2, r3 = refs[n_weights : n_weights + 5]
    outs = refs[n_weights + 5 :]
    rows, width = outs[0].shape
    tn = (((0,), (0,)), ((), ()))
    step = min(width, 512)

    @pl.loop(0, width // step)
    def _(i):
        cols = pl.ds(pl.multiple_of(i * step, step), step)
        total = None
        for w in weights:
            for k in range(4):
                if k == 0:
                    values = jnp.concatenate([own[:BLK, cols], exchanged[:BLK, cols]], axis=0)
                else:
                    values = (r1, r2, r3)[k - 1][:, cols]
                part = lax.dot_general(w[k], values, tn, preferred_element_type=F32)
                total = part if total is None else total + part
        total = total.astype(BF)
        for w, out in enumerate(outs):
            out[:, cols] = total[w * rows : (w + 1) * rows, :]


def combine(weights, own, exchanged, returned, rows):
    width = own.shape[1]
    flops = len(weights) * 2 * 8 * BLK * WIN * rows * width
    return call(
        functools.partial(combine_kernel, len(weights)),
        tuple([sds((rows, width))] * 4), flops, (*weights, own, exchanged, *returned),
    )


def expert_a_kernel(a0, a1, a2, a3, ao, c0, c1, c2, c3, co, perm, w_gu, w_dn, rows_in, rows_scaled, both, hidden, cots):
    half = 4 * BLK
    width = a0.shape[1]
    ff = w_dn.shape[1]
    for k, (a, c) in enumerate(((a0, c0), (a1, c1), (a2, c2), (a3, c3))):
        rows_in[k * BLK : (k + 1) * BLK, :] = a[:BLK, :]
        cots[k * BLK : (k + 1) * BLK, :] = c[:BLK, :]
    rows_in[half:, :] = ao[...]
    cots[half:, :] = co[...]
    wide = min(512, width)

    @pl.loop(0, width // wide)
    def _(i):
        cols = pl.ds(pl.multiple_of(i * wide, wide), wide)
        for h in range(2):
            rs = slice(h * half, (h + 1) * half)
            rows_scaled[rs, cols] = jnp.dot(perm[...], cots[rs, cols], preferred_element_type=F32).astype(BF)

    step = min(256, ff)

    @pl.loop(0, ff // step)
    def _(i):
        gc = pl.ds(pl.multiple_of(i * step, step), step)
        uc = pl.ds(pl.multiple_of(ff + i * step, step), step)
        g = jnp.dot(rows_in[...], w_gu[:, gc], preferred_element_type=F32)
        u = jnp.dot(rows_in[...], w_gu[:, uc], preferred_element_type=F32)
        grad = jnp.dot(rows_scaled[...], w_dn[:, gc], preferred_element_type=F32)
        s = jax.nn.sigmoid(g)
        active = g * s
        hidden[:, gc] = (active * u).astype(BF)
        both[:, gc] = (grad * u * s * (1.0 + g * (1.0 - s))).astype(BF)
        both[:, uc] = (grad * active).astype(BF)


def row_grad_kernel(both, w_gu, own, other):
    half = 4 * BLK
    width = w_gu.shape[0]
    step = min(256, width)
    nt = (((1,), (1,)), ((), ()))

    @pl.loop(0, width // step)
    def _(i):
        cols = pl.ds(pl.multiple_of(i * step, step), step)
        for h, out in enumerate((own, other)):
            rs = slice(h * half, (h + 1) * half)
            out[:, cols] = lax.dot_general(both[rs, :], w_gu[cols, :], nt, preferred_element_type=F32).astype(BF)


def grad_kernel(chunk_ids, rows_in, rows_scaled, both, hidden, g0, g1, g2, g3):
    deep = g0.shape[0]
    wide = both.shape[1]
    tn = (((0,), (0,)), ((), ()))
    for j, out in enumerate((g0, g1, g2, g3)):
        cols = pl.ds(pl.multiple_of(chunk_ids[j] * deep, deep), deep)
        out[:, :wide] = lax.dot_general(rows_in[:, cols], both[...], tn, preferred_element_type=F32).astype(BF)
        out[:, wide:] = lax.dot_general(rows_scaled[:, cols], hidden[...], tn, preferred_element_type=F32).astype(BF)


def expert_b_kernel(b0, b1, b2, b3, bo, w_gu, w_dn, own, other, rows_in, hidden):
    half = 4 * BLK
    width = b0.shape[1]
    ff = w_dn.shape[1]
    for k, b in enumerate((b0, b1, b2, b3)):
        rows_in[k * BLK : (k + 1) * BLK, :] = b[:BLK, :]
    rows_in[half:, :] = bo[...]
    step = min(256, ff)

    @pl.loop(0, ff // step)
    def _(i):
        gc = pl.ds(pl.multiple_of(i * step, step), step)
        uc = pl.ds(pl.multiple_of(ff + i * step, step), step)
        g = jnp.dot(rows_in[...], w_gu[:, gc], preferred_element_type=F32)
        u = jnp.dot(rows_in[...], w_gu[:, uc], preferred_element_type=F32)
        hidden[:, gc] = (g * jax.nn.sigmoid(g) * u).astype(BF)

    nt = (((1,), (1,)), ((), ()))
    wide = min(256, width)

    @pl.loop(0, width // wide)
    def _(i):
        cols = pl.ds(pl.multiple_of(i * wide, wide), wide)
        res = lax.dot_general(hidden[...], w_dn[cols, :], nt, preferred_element_type=F32).astype(BF)
        own[:, cols] = res[:half]
        other[:, cols] = res[half:]


def gather_window(shift, block):
    return (block, shift(block, 1), shift(block, 2), shift(block, 3))


def send_rows(shift, rows, first=None, late=()):
    near = shift(rows[1], 1)
    last = rows[3] if late is None else after(rows[3], near, *late)
    got = (rows[0], near, shift(rows[2], 2), shift(last, 3))
    far = got if first is None else tuple(lax.optimization_barrier((*got, first))[:4])
    other = swap_core(jnp.concatenate([r[BLK:] for r in far], axis=0))
    return got, other


def pair_rows(own, other):
    exchanged = swap_core(other)
    pairs = []
    for k in (1, 2, 3):
        rs = slice(k * BLK, (k + 1) * BLK)
        pairs.append(jnp.concatenate([own[rs], exchanged[rs]], axis=0))
    return exchanged, pairs


def return_rows(shift, pairs):
    near = shift(pairs[0], 1, True)
    return near, shift(pairs[1], 2, True), shift(after(pairs[2], near), 3, True)


def return_window(shift, parts):
    total = parts[0].astype(F32)
    for k in (1, 2, 3):
        total = total + shift(parts[k], k, True).astype(F32)
    return total.astype(BF)


def reduce_y(chunks, first=None, relay_first=None):
    relayed = shift_y(chunks[2], 1)
    direct = shift_y(chunks[3] if first is None else after(chunks[3], first), 3)
    mine = chunks[1] if relay_first is None else after(chunks[1], relay_first)
    summed = shift_y((mine.astype(F32) + relayed.astype(F32)).astype(BF), 1)
    return chunks[0].astype(F32) + direct.astype(F32) + summed.astype(F32), direct, summed


def body(tokens_a, cotangent_a, route_a, gate_a, tokens_b, route_b, gate_b, w_gate_up, w_down):
    rows, width = tokens_a.shape
    w_gu, w_dn = w_gate_up[0], w_down[0]
    ff = w_dn.shape[1]
    x, zl, c = lax.axis_index("x"), lax.axis_index("zl"), lax.axis_index("c")
    zh, y = lax.axis_index("zh"), lax.axis_index("y")
    s = 1 - 2 * c
    k8 = jnp.arange(8, dtype=jnp.int32) // 2
    c8 = c ^ (jnp.arange(8, dtype=jnp.int32) & 1)
    ids_x = (((x + s * k8) & 3) * 4 + zl) * 2 + c8
    ids_z = (x * 4 + ((zl + s * k8) & 3)) * 2 + c8
    k4 = (y + s * jnp.arange(4, dtype=jnp.int32)) & 3
    chunks_far = (1 - zh) * 4 + k4
    chunks_near = zh * 4 + k4

    stacked = jnp.concatenate([route_a.T.astype(F32), gate_a.T, route_b.T.astype(F32), gate_b.T], axis=0)
    code_a, code_b = call(code_kernel, (sds((rows, PAD)),) * 2, 0, (stacked,), mib=2)
    win_ab = gather_window(shift_z, jnp.concatenate([tokens_a, code_a, tokens_b, code_b], axis=1))
    win_c = gather_window(shift_x, jnp.concatenate([cotangent_a, code_a], axis=1))
    (rows_a, keep_a), (rows_c, _), (rows_b, keep_b) = dispatch(
        (ids_x, ids_z, ids_x), (win_ab, win_c), (("plain", 0, 0), ("scaled", 1, 0), ("gated", 0, 1)), width
    )
    got_a, other_a = send_rows(shift_x, rows_a)
    got_c, other_c = send_rows(shift_z, rows_c)

    half = 4 * BLK
    i = jnp.arange(half, dtype=jnp.int32)
    source = ((i % BLK) // CAP) * BLK + (i // BLK) * CAP + i % CAP
    perm = (source[:, None] == i[None, :]).astype(BF)
    rows_in, rows_scaled, both, hidden = call(
        expert_a_kernel,
        (sds((2 * half, width)), sds((2 * half, width)), sds((2 * half, 2 * ff)), sds((2 * half, ff))),
        2 * 2 * half * width * 3 * ff,
        (*got_a, other_a, *got_c, other_c, perm, w_gu, w_dn),
        [pltpu.VMEM((2 * half, width), BF)], mib=9,
    )
    chunk = sds((width // 8, 3 * ff))
    grad_flops = 2 * 2 * half * width // 2 * 3 * ff
    operands = (rows_in, rows_scaled, both, hidden)
    own_a, back_a = call(
        row_grad_kernel, (sds((half, width)),) * 2, 2 * 2 * half * width * 2 * ff, (both, w_gu)
    )
    far = call(grad_kernel, (chunk,) * 4, grad_flops, (after(chunks_far, back_a), *operands), smem=1)
    exchanged_a, pairs_a = pair_rows(own_a, back_a)
    got_b, other_b = send_rows(shift_x, after(rows_b, got_a[2]), far, None)
    far_sum, direct, summed = reduce_y(far, relay_first=pairs_a)
    near = call(grad_kernel, (chunk,) * 4, grad_flops, (after(chunks_near, far), *operands), smem=1)
    far_total = swap_zh(far_sum.astype(BF))

    returned_a = return_rows(shift_x, pairs_a)
    own_b, back_b = call(
        expert_b_kernel, (sds((half, width)),) * 2, 2 * 2 * half * width * 3 * ff,
        (*got_b, after(other_b, near, pairs_a), w_gu, w_dn),
        [pltpu.VMEM((2 * half, width), BF), pltpu.VMEM((2 * half, ff), BF)], mib=9,
    )
    exchanged_b, pairs_b = pair_rows(own_b, back_b)
    returned_b = return_rows(shift_x, after(pairs_b, returned_a[0], returned_a[1]))
    near_total, _, _ = reduce_y(after(near, direct), (summed, returned_a[2]))
    input_grad = return_window(shift_z, combine(keep_a, after(own_a, far_total, returned_b[0], returned_b[1]), exchanged_a, returned_a, rows))
    mixed = return_window(shift_z, combine(keep_b, own_b, exchanged_b, returned_b, rows))
    grads = near_total + far_total.astype(F32)
    return (input_grad, mixed, grads[None, :, : 2 * ff], grads[None, :, 2 * ff :])


def solution(mesh):
    fine = Mesh(mesh.devices.reshape(SIZES), AXES)
    tokens = P(AXES, None)
    return jax.shard_map(
        body,
        mesh=fine,
        in_specs=(tokens,) * 7 + (P(("x", "zl", "c"), None, None),) * 2,
        out_specs=(tokens, tokens) + (P(("x", "zl", "c"), ("zh", "y"), None),) * 2,
        check_vma=False,
    )
```

```python
import functools

import jax
import jax.numpy as jnp
from jax import lax
from jax.experimental import pallas as pl
from jax.experimental.pallas import tpu as pltpu
from jax.sharding import Mesh, PartitionSpec as P

AXES = ("x", "zl", "c", "zh", "y")
SIZES = (4, 4, 2, 2, 4)
BF = jnp.bfloat16
F32 = jnp.float32
PAD = 128
CAP = 20
WIN = 4
BLK = WIN * CAP
KEEP = {"plain": 1, "scaled": 0, "gated": 2}
MIB = 1024 * 1024


def shift_x(value, k, back=False):
    perm = []
    for x in range(4):
        for c in range(2):
            s = (1 if c == 0 else -1) * (-1 if back else 1)
            perm.append((x * 2 + c, ((x + s * k) % 4) * 2 + c))
    return lax.ppermute(value, ("x", "c"), perm)


def shift_z(value, k, back=False):
    step = -1 if k == 3 else k
    perm = []
    for z in range(8):
        for c in range(2):
            s = (1 if c == 0 else -1) * (-1 if back else 1)
            to = (z + s * step) % 8
            perm.append((((z % 4) * 2 + c) * 2 + z // 4, ((to % 4) * 2 + c) * 2 + to // 4))
    return lax.ppermute(value, ("zl", "c", "zh"), perm)


def shift_y(value, k):
    perm = []
    for c in range(2):
        for y in range(4):
            s = 1 if c == 0 else -1
            perm.append((c * 4 + y, c * 4 + (y + s * k) % 4))
    return lax.ppermute(value, ("c", "y"), perm)


def swap_core(value):
    return lax.ppermute(value, "c", [(0, 1), (1, 0)])


def swap_zh(value):
    return lax.ppermute(value, "zh", [(0, 1), (1, 0)])


def call(kernel, out_shape, flops, operands, scratch=(), smem=0, mib=10):
    nbytes = sum(o.size * o.dtype.itemsize for o in operands)
    nbytes += sum(o.size * o.dtype.itemsize for o in jax.tree.leaves(out_shape))
    vmem = pl.BlockSpec(memory_space=pltpu.VMEM)
    specs = [pl.BlockSpec(memory_space=pltpu.SMEM)] * smem
    specs += [vmem] * (len(operands) - smem)
    return pl.pallas_call(
        kernel,
        out_shape=out_shape,
        in_specs=specs,
        out_specs=jax.tree.map(lambda _: vmem, out_shape),
        scratch_shapes=list(scratch),
        compiler_params=pltpu.CompilerParams(vmem_limit_bytes=mib * MIB),
        cost_estimate=pl.CostEstimate(flops=flops, bytes_accessed=nbytes, transcendentals=0),
    )(*operands)


def after(value, *others):
    return lax.optimization_barrier((value, *others))[0]


def sds(shape, dtype=BF):
    return jax.ShapeDtypeStruct(shape, dtype)


def code_kernel(stacked, code_a, code_b):
    top = stacked.shape[0] // 4
    rows = stacked.shape[1]
    sub = lax.broadcasted_iota(jnp.int32, (PAD, rows), 0)
    expert = (sub & 31).astype(F32)
    for at, out in ((0, code_a), (2 * top, code_b)):
        value = jnp.zeros((PAD, rows), F32)
        mask = jnp.zeros((PAD, rows), F32)
        for k in range(at, at + top):
            hit = stacked[k : k + 1, :] == expert
            value = jnp.where(hit, stacked[k + top : k + top + 1, :], value)
            mask = jnp.where(hit, 1.0, mask)
        first = value.astype(BF).astype(F32)
        second = (value - first).astype(BF).astype(F32)
        third = value - first - second
        coded = jnp.where(sub < 32, first, jnp.where(sub < 64, second, third))
        out[...] = jnp.where(sub < 96, coded, mask).T.astype(BF)


def dispatch_kernel(jobs, *refs):
    n = len(jobs)
    ids, refs = refs[:n], refs[n:]
    windows = 1 + max(window for _, window, _ in jobs)
    blocks, outs, toks = refs[: WIN * windows], refs[WIN * windows : -1], refs[-1]
    for j, (kind, window, at) in enumerate(jobs):
        keep = KEEP[kind]
        near = blocks[WIN * window : WIN * window + WIN]
        pick_rows(kind, ids[j], near, at * (toks.shape[1] + PAD), outs[:4], outs[4 : 4 + keep], toks)
        outs = outs[4 + keep :]


def pick_rows(kind, ids, blocks, start, outs, weights, toks):
    scaled, gated = kind == "scaled", kind == "gated"
    rows, width = blocks[0].shape[0], toks.shape[1]
    stop = start + width
    n = WIN * rows
    for w, block in enumerate(blocks):
        toks[w * rows : (w + 1) * rows, :] = block[:, start:stop]
    code = jnp.concatenate([block[:, stop : stop + PAD] for block in blocks], axis=0)
    sub = lax.broadcasted_iota(jnp.int32, (16, PAD), 0)
    lane = lax.broadcasted_iota(jnp.int32, (16, PAD), 1)
    wanted = jnp.full((16, PAD), -1, jnp.int32)
    for j in range(8):
        wanted = jnp.where(sub == j, ids[j], wanted)
    hit = (lane & 31) == wanted
    nt = (((1,), (1,)), ((), ()))
    pick_gate = jnp.where(hit & (lane < 96), 1.0, 0.0).astype(BF)
    pick_mask = jnp.where(hit & (lane >= 96), 1.0, 0.0).astype(BF)
    gate = lax.dot_general(pick_gate, code, nt, preferred_element_type=F32)
    mask = lax.dot_general(pick_mask, code, nt, preferred_element_type=F32)
    ahead = lax.broadcasted_iota(jnp.int32, (n, n), 0)
    here = lax.broadcasted_iota(jnp.int32, (n, n), 1)
    before = jnp.where((ahead < here) & (ahead // rows == here // rows), 1.0, 0.0).astype(BF)
    rank = jnp.dot(mask.astype(BF), before, preferred_element_type=F32)
    column = lax.broadcasted_iota(jnp.int32, (16, n), 1)
    other = lax.broadcasted_iota(jnp.int32, (16, n), 0) & 1
    slot = rank.astype(jnp.int32) + (column // rows) * CAP + other * BLK
    slot = jnp.where(mask > 0.5, slot, -1)
    place = lax.broadcasted_iota(jnp.int32, (2 * BLK, n), 0)
    for k, out in enumerate(outs):
        near = place == slot[2 * k : 2 * k + 1, :]
        far = place == slot[2 * k + 1 : 2 * k + 2, :]
        choice = jnp.where(near | far, 1.0, 0.0).astype(BF)
        if scaled or gated:
            gates = jnp.where(near, gate[2 * k : 2 * k + 1, :], 0.0)
            gates = jnp.where(far, gate[2 * k + 1 : 2 * k + 2, :], gates)
        if gated:
            high = gates.astype(BF)
            weights[0][k] = high
            weights[1][k] = (gates - high.astype(F32)).astype(BF)
        elif weights:
            weights[0][k] = choice
        picked = jnp.dot(choice, toks[...], preferred_element_type=F32)
        if scaled:
            picked = picked * jnp.sum(gates, axis=1, keepdims=True)
        out[...] = picked.astype(BF)


def dispatch(ids, windows, jobs, width):
    n = WIN * windows[0][0].shape[0]
    out, counts = [], []
    for kind, _, _ in jobs:
        out += [sds((2 * BLK, width))] * 4 + [sds((4, 2 * BLK, n))] * KEEP[kind]
        counts.append(4 + KEEP[kind])
    flops = 2 * 8 * BLK * n * width * len(jobs)
    blocks = [block for window in windows for block in window]
    res = call(
        functools.partial(dispatch_kernel, jobs), tuple(out), flops,
        (*ids, *blocks), [pltpu.VMEM((n, width), BF)], smem=len(jobs), mib=8,
    )
    parts = []
    for count in counts:
        parts.append((res[:4], res[4:count]))
        res = res[count:]
    return parts


def combine_kernel(n_weights, *refs):
    weights = refs[:n_weights]
    own, exchanged, r1, r2, r3 = refs[n_weights : n_weights + 5]
    outs = refs[n_weights + 5 :]
    rows, width = outs[0].shape
    tn = (((0,), (0,)), ((), ()))
    step = min(width, 512)

    @pl.loop(0, width // step)
    def _(i):
        cols = pl.ds(pl.multiple_of(i * step, step), step)
        total = None
        for w in weights:
            for k in range(4):
                if k == 0:
                    values = jnp.concatenate([own[:BLK, cols], exchanged[:BLK, cols]], axis=0)
                else:
                    values = (r1, r2, r3)[k - 1][:, cols]
                part = lax.dot_general(w[k], values, tn, preferred_element_type=F32)
                total = part if total is None else total + part
        total = total.astype(BF)
        for w, out in enumerate(outs):
            out[:, cols] = total[w * rows : (w + 1) * rows, :]


def combine(weights, own, exchanged, returned, rows):
    width = own.shape[1]
    flops = len(weights) * 2 * 8 * BLK * WIN * rows * width
    return call(
        functools.partial(combine_kernel, len(weights)),
        tuple([sds((rows, width))] * 4), flops, (*weights, own, exchanged, *returned),
    )


def expert_a_kernel(a0, a1, a2, a3, ao, c0, c1, c2, c3, co, perm, w_gu, w_dn, rows_in, rows_scaled, both, hidden, cots):
    half = 4 * BLK
    width = a0.shape[1]
    ff = w_dn.shape[1]
    for k, (a, c) in enumerate(((a0, c0), (a1, c1), (a2, c2), (a3, c3))):
        rows_in[k * BLK : (k + 1) * BLK, :] = a[:BLK, :]
        cots[k * BLK : (k + 1) * BLK, :] = c[:BLK, :]
    rows_in[half:, :] = ao[...]
    cots[half:, :] = co[...]
    wide = min(512, width)

    @pl.loop(0, width // wide)
    def _(i):
        cols = pl.ds(pl.multiple_of(i * wide, wide), wide)
        for h in range(2):
            rs = slice(h * half, (h + 1) * half)
            rows_scaled[rs, cols] = jnp.dot(perm[...], cots[rs, cols], preferred_element_type=F32).astype(BF)

    step = min(256, ff)

    @pl.loop(0, ff // step)
    def _(i):
        gc = pl.ds(pl.multiple_of(i * step, step), step)
        uc = pl.ds(pl.multiple_of(ff + i * step, step), step)
        g = jnp.dot(rows_in[...], w_gu[:, gc], preferred_element_type=F32)
        u = jnp.dot(rows_in[...], w_gu[:, uc], preferred_element_type=F32)
        grad = jnp.dot(rows_scaled[...], w_dn[:, gc], preferred_element_type=F32)
        s = jax.nn.sigmoid(g)
        active = g * s
        hidden[:, gc] = (active * u).astype(BF)
        both[:, gc] = (grad * u * s * (1.0 + g * (1.0 - s))).astype(BF)
        both[:, uc] = (grad * active).astype(BF)


def row_grad_kernel(both, w_gu, own, other):
    half = 4 * BLK
    width = w_gu.shape[0]
    step = min(256, width)
    nt = (((1,), (1,)), ((), ()))

    @pl.loop(0, width // step)
    def _(i):
        cols = pl.ds(pl.multiple_of(i * step, step), step)
        for h, out in enumerate((own, other)):
            rs = slice(h * half, (h + 1) * half)
            out[:, cols] = lax.dot_general(both[rs, :], w_gu[cols, :], nt, preferred_element_type=F32).astype(BF)


def grad_kernel(chunk_ids, rows_in, rows_scaled, both, hidden, g0, g1, g2, g3):
    deep = g0.shape[0]
    wide = both.shape[1]
    tn = (((0,), (0,)), ((), ()))
    for j, out in enumerate((g0, g1, g2, g3)):
        cols = pl.ds(pl.multiple_of(chunk_ids[j] * deep, deep), deep)
        out[:, :wide] = lax.dot_general(rows_in[:, cols], both[...], tn, preferred_element_type=F32).astype(BF)
        out[:, wide:] = lax.dot_general(rows_scaled[:, cols], hidden[...], tn, preferred_element_type=F32).astype(BF)


def expert_b_kernel(b0, b1, b2, b3, bo, w_gu, w_dn, own, other, rows_in, hidden):
    half = 4 * BLK
    width = b0.shape[1]
    ff = w_dn.shape[1]
    for k, b in enumerate((b0, b1, b2, b3)):
        rows_in[k * BLK : (k + 1) * BLK, :] = b[:BLK, :]
    rows_in[half:, :] = bo[...]
    step = min(256, ff)

    @pl.loop(0, ff // step)
    def _(i):
        gc = pl.ds(pl.multiple_of(i * step, step), step)
        uc = pl.ds(pl.multiple_of(ff + i * step, step), step)
        g = jnp.dot(rows_in[...], w_gu[:, gc], preferred_element_type=F32)
        u = jnp.dot(rows_in[...], w_gu[:, uc], preferred_element_type=F32)
        hidden[:, gc] = (g * jax.nn.sigmoid(g) * u).astype(BF)

    nt = (((1,), (1,)), ((), ()))
    wide = min(256, width)

    @pl.loop(0, width // wide)
    def _(i):
        cols = pl.ds(pl.multiple_of(i * wide, wide), wide)
        res = lax.dot_general(hidden[...], w_dn[cols, :], nt, preferred_element_type=F32).astype(BF)
        own[:, cols] = res[:half]
        other[:, cols] = res[half:]


def gather_window(shift, block):
    return (block, shift(block, 1), shift(block, 2), shift(block, 3))


def send_rows(shift, rows, first=None, late=()):
    near = shift(rows[1], 1)
    last = rows[3] if late is None else after(rows[3], near, *late)
    got = (rows[0], near, shift(rows[2], 2), shift(last, 3))
    far = got if first is None else tuple(lax.optimization_barrier((*got, first))[:4])
    other = swap_core(jnp.concatenate([r[BLK:] for r in far], axis=0))
    return got, other


def pair_rows(own, other):
    exchanged = swap_core(other)
    pairs = []
    for k in (1, 2, 3):
        rs = slice(k * BLK, (k + 1) * BLK)
        pairs.append(jnp.concatenate([own[rs], exchanged[rs]], axis=0))
    return exchanged, pairs


def return_rows(shift, pairs):
    near = shift(pairs[0], 1, True)
    return near, shift(pairs[1], 2, True), shift(after(pairs[2], near), 3, True)


def return_window(shift, parts):
    total = parts[0].astype(F32)
    for k in (1, 2, 3):
        total = total + shift(parts[k], k, True).astype(F32)
    return total.astype(BF)


def reduce_y(chunks, first=None, relay_first=None):
    relayed = shift_y(chunks[2], 1)
    direct = shift_y(chunks[3] if first is None else after(chunks[3], first), 3)
    mine = chunks[1] if relay_first is None else after(chunks[1], relay_first)
    summed = shift_y((mine.astype(F32) + relayed.astype(F32)).astype(BF), 1)
    return chunks[0].astype(F32) + direct.astype(F32) + summed.astype(F32), direct, summed


def body(tokens_a, cotangent_a, route_a, gate_a, tokens_b, route_b, gate_b, w_gate_up, w_down):
    rows, width = tokens_a.shape
    w_gu, w_dn = w_gate_up[0], w_down[0]
    ff = w_dn.shape[1]
    x, zl, c = lax.axis_index("x"), lax.axis_index("zl"), lax.axis_index("c")
    zh, y = lax.axis_index("zh"), lax.axis_index("y")
    s = 1 - 2 * c
    k8 = jnp.arange(8, dtype=jnp.int32) // 2
    c8 = c ^ (jnp.arange(8, dtype=jnp.int32) & 1)
    ids_x = (((x + s * k8) & 3) * 4 + zl) * 2 + c8
    ids_z = (x * 4 + ((zl + s * k8) & 3)) * 2 + c8
    k4 = (y + s * jnp.arange(4, dtype=jnp.int32)) & 3
    chunks_far = (1 - zh) * 4 + k4
    chunks_near = zh * 4 + k4

    stacked = jnp.concatenate([route_a.T.astype(F32), gate_a.T, route_b.T.astype(F32), gate_b.T], axis=0)
    code_a, code_b = call(code_kernel, (sds((rows, PAD)),) * 2, 0, (stacked,), mib=2)
    win_ab = gather_window(shift_z, jnp.concatenate([tokens_a, code_a, tokens_b, code_b], axis=1))
    win_c = gather_window(shift_x, jnp.concatenate([cotangent_a, code_a], axis=1))
    (rows_a, keep_a), (rows_c, _), (rows_b, keep_b) = dispatch(
        (ids_x, ids_z, ids_x), (win_ab, win_c), (("plain", 0, 0), ("scaled", 1, 0), ("gated", 0, 1)), width
    )
    got_a, other_a = send_rows(shift_x, rows_a)
    got_c, other_c = send_rows(shift_z, rows_c)

    half = 4 * BLK
    i = jnp.arange(half, dtype=jnp.int32)
    source = ((i % BLK) // CAP) * BLK + (i // BLK) * CAP + i % CAP
    perm = (source[:, None] == i[None, :]).astype(BF)
    rows_in, rows_scaled, both, hidden = call(
        expert_a_kernel,
        (sds((2 * half, width)), sds((2 * half, width)), sds((2 * half, 2 * ff)), sds((2 * half, ff))),
        2 * 2 * half * width * 3 * ff,
        (*got_a, other_a, *got_c, other_c, perm, w_gu, w_dn),
        [pltpu.VMEM((2 * half, width), BF)], mib=9,
    )
    chunk = sds((width // 8, 3 * ff))
    grad_flops = 2 * 2 * half * width // 2 * 3 * ff
    operands = (rows_in, rows_scaled, both, hidden)
    own_a, back_a = call(
        row_grad_kernel, (sds((half, width)),) * 2, 2 * 2 * half * width * 2 * ff, (both, w_gu)
    )
    far = call(grad_kernel, (chunk,) * 4, grad_flops, (after(chunks_far, back_a), *operands), smem=1)
    exchanged_a, pairs_a = pair_rows(own_a, back_a)
    got_b, other_b = send_rows(shift_x, after(rows_b, got_a[2]), far, None)
    far_sum, direct, summed = reduce_y(far, relay_first=pairs_a)
    near = call(grad_kernel, (chunk,) * 4, grad_flops, (after(chunks_near, far), *operands), smem=1)
    near_total, _, _ = reduce_y(after(near, direct), summed)
    far_total = swap_zh(far_sum.astype(BF))

    returned_a = return_rows(shift_x, pairs_a)
    own_b, back_b = call(
        expert_b_kernel, (sds((half, width)),) * 2, 2 * 2 * half * width * 3 * ff,
        (*got_b, after(other_b, near, pairs_a), w_gu, w_dn),
        [pltpu.VMEM((2 * half, width), BF), pltpu.VMEM((2 * half, ff), BF)], mib=9,
    )
    exchanged_b, pairs_b = pair_rows(own_b, back_b)
    returned_b = return_rows(shift_x, after(pairs_b, returned_a[0], returned_a[1]))
    input_grad = return_window(shift_z, combine(keep_a, after(own_a, far_total, returned_b[0]), exchanged_a, returned_a, rows))
    mixed = return_window(shift_z, combine(keep_b, own_b, exchanged_b, returned_b, rows))
    grads = near_total + far_total.astype(F32)
    return (input_grad, mixed, grads[None, :, : 2 * ff], grads[None, :, 2 * ff :])


def solution(mesh):
    fine = Mesh(mesh.devices.reshape(SIZES), AXES)
    tokens = P(AXES, None)
    return jax.shard_map(
        body,
        mesh=fine,
        in_specs=(tokens,) * 7 + (P(("x", "zl", "c"), None, None),) * 2,
        out_specs=(tokens, tokens) + (P(("x", "zl", "c"), ("zh", "y"), None),) * 2,
        check_vma=False,
    )
```
